32 devices in a mesh: groups: 2 (over y), blk: 4 (over z), heads: 2 (over x), sub: 2 (over core).
Axes of the slice: x: 2, y: 2, z: 4, core: 2. Of those that a mesh axis runs over, the one named last changes fastest.
Arguments:
- queries: bfloat16 [512, 4096], P(('groups', 'blk'), ('heads', 'sub')), parts along dimension 0, may hold values from -3 to 3
- keys: bfloat16 [16384, 4096], P(('groups', 'blk'), ('heads', 'sub')), parts along dimension 0, may hold values from -3 to 3
- values: bfloat16 [16384, 4096], P(('groups', 'blk'), ('heads', 'sub')), parts along dimension 0, may hold values from -6 to 6
- out_weight: bfloat16 [4096, 4096], P(('heads', 'sub')), may hold values from -0.125 to 0.125
- counts: int32 [32], P('groups'), parts along dimension 0, may hold values from 1 to 16, 32 in all
- slot_of: int32 [64], P('groups'), parts along dimension 0, may hold values from 0 to 31, each once
- beam_request: int32 [512], P('groups'), parts along dimension 0, may hold values from 0 to 15, as said below
Outputs:
- mixed: bfloat16 [512, 4096], P(('groups', 'blk'), ('heads', 'sub')), parts along dimension 0
The draws below stay inside these ranges and needn't reach their ends.
There are 2 independent parts, one for each index of `groups`. The reference program is written for one: setup_inputs(seed, part) draws one part's arguments, and reference() takes and returns one part's arrays. A program takes and returns all parts, laid end to end along the dimension named above; an argument that names none is the same for every part. Nothing has to cross between parts.
Inputs may be any that keep to these rules, and one draw needn't show every extreme that they name: `beam_request`: the beams of each request are 16 consecutive rows starting at a multiple of 16; each request is named by exactly 16 beams.
All inputs are finite; a program needn't handle non-finite values.
Results may differ from the reference program's by a relative error of at most 0.012.
Values may be sent and summed in bfloat16 or wider, within the bound.
A program may use at most 64 MiB of HBM per device.

```python
import math
import jax
import jax.numpy as jnp
import numpy as np
from jax import lax

D = 4096
HEAD_COUNT = 64
HEAD_DIM = 64
BEAMS = 16
PLEN = 256
MAXP = 16
ROWS = 256
REQS = 16
PASSAGES = 32
KEYS = 8192
INNER = 4096


def draw_queries(key, part):
    key = jax.random.fold_in(key, 11)
    result = 0.35 * jax.random.truncated_normal(key, -8.0, 8.0, (ROWS, INNER), jnp.float32)
    return result.astype(jnp.bfloat16)


def draw_keys(key, part):
    key = jax.random.fold_in(key, 23)
    result = 0.35 * jax.random.truncated_normal(key, -8.0, 8.0, (KEYS, INNER), jnp.float32)
    return result.astype(jnp.bfloat16)


def draw_beam_request(key, part):
    key = jax.random.fold_in(key, 5)
    order = jax.random.permutation(key, REQS)
    return jnp.repeat(order, BEAMS).astype(jnp.int32)


def raised(entries, stream_key, source, target, parts, factor):
    owner, partner = [(jnp.arange(entries.shape[dim]) // (entries.shape[dim] // parts)).reshape([-1 if axis == dim else 1 for axis in range(entries.ndim)]) for dim in (source, target)]
    chosen = jax.random.permutation(stream_key, parts)[partner]
    strong = (owner == chosen) | (owner == (partner + parts // 2) % parts)
    return jnp.where(strong, factor * entries, entries)


def block_levels(rng, shape, cuts, low, top_value):
    loudness = 1.0
    for position, blocks in cuts:
        draws = jax.random.uniform(jax.random.fold_in(jax.random.fold_in(rng, 6), position), (blocks,), jnp.float32, low / len(cuts), top_value / len(cuts))
        loudness = loudness * jnp.repeat(jnp.exp(draws), shape[position] // blocks).reshape((-1,) + (1,) * (len(shape) - 1 - position))
    return loudness


def length_profile(count, total, reach, slope):
    weights = [(1 << 20) // math.isqrt(standing ** slope) + 1 for standing in range(2, count + 1)]
    spare, given = total - reach - (count - 1), [1] * (count - 1)
    while spare > 0:
        movable = [i for i in range(count - 1) if given[i] < reach]
        pool, budget = sum([weights[i] for i in movable]), spare
        for i in movable:
            extra = min(reach - given[i], max(1, budget * weights[i] // pool), spare)
            given[i] = given[i] + extra
            spare = spare - extra
    return np.array([reach] + given)


def uneven_parts(rng, count, total, reach, slope):
    if count == 2:
        one = jax.random.randint(rng, (), max(1, total - reach), min(reach, total - 1) + 1)
        return jnp.stack([one, total - one])
    sizes = jnp.asarray(length_profile(count, total, reach, slope), jnp.int32)
    pairs = (count - 1) // 2
    giver, receiver = sizes[1:1 + 2 * pairs:2], sizes[2:2 + 2 * pairs:2]
    slack = jnp.minimum(giver - 1, reach - receiver)
    shifted = jax.random.randint(jax.random.fold_in(rng, 1), (pairs,), 0, 1 << 20) % (slack + 1)
    sizes = sizes.at[1:1 + 2 * pairs:2].set(giver - shifted).at[2:2 + 2 * pairs:2].set(receiver + shifted)
    return sizes[jax.random.permutation(jax.random.fold_in(rng, 2), count)]


def noise(own_key, extent, spread, reach, split=(), kind=jnp.bfloat16):
    values = spread * jax.random.normal(own_key, extent, jnp.float32)
    if split:
        values = values * block_levels(own_key, extent, split, -0.22, 0.18)
    return jnp.clip(values, -reach, reach).astype(kind)


def gaussian_with(stream_key, shape, deviation, reach, shards, heavy, kind=jnp.bfloat16):
    drawn = deviation * jax.random.normal(stream_key, shape, jnp.float32)
    if shards:
        drawn = drawn * block_levels(stream_key, shape, shards, -0.22, 0.18)
    return jnp.clip(raised(drawn, jax.random.fold_in(stream_key, 3), *heavy), -reach, reach).astype(kind)


def setup_inputs(seed: int = 0, part: int = 0) -> dict:
    seeds = jax.random.split(jax.random.key(seed), 8)
    part_splits = jax.random.split(jax.random.fold_in(seeds[7], part), 8)
    queries = draw_queries(jax.random.fold_in(jax.random.fold_in(seeds[7], part), 71), part)
    keys = draw_keys(jax.random.fold_in(jax.random.fold_in(seeds[7], part), 71), part)
    values = noise(part_splits[2], (KEYS, INNER), 1.0, 6.0, ((0, 4), (1, 4)))
    out_weight = gaussian_with(seeds[3], (INNER, D), INNER ** -0.5, 0.125, ((0, 4),), (0, 1, 4, 2.0))
    counts = uneven_parts(part_splits[4], REQS, PASSAGES, MAXP, 2).astype(jnp.int32)
    slot_of = jax.random.permutation(part_splits[5], PASSAGES).astype(jnp.int32)
    beam_request = draw_beam_request(jax.random.fold_in(jax.random.fold_in(seeds[7], part), 71), part)
    return dict(queries=queries, keys=keys, values=values, out_weight=out_weight, counts=counts, slot_of=slot_of, beam_request=beam_request)


floor_score = -1.0e30


def reference(queries, keys, values, out_weight, counts, slot_of, beam_request):
    passage = jnp.arange(PASSAGES, dtype=jnp.int32)
    ends = jnp.cumsum(counts).astype(jnp.int32)
    owner = jnp.sum((passage[:, None] >= ends[None, :]).astype(jnp.int32), axis=1).astype(jnp.int32)
    slot_owner = jnp.zeros((PASSAGES,), jnp.int32).at[slot_of].set(owner)
    key_request = jnp.repeat(slot_owner, PLEN)
    valid = beam_request[:, None] == key_request[None, :]
    query_heads = queries.reshape(ROWS, HEAD_COUNT, HEAD_DIM).transpose(1, 0, 2)
    key_heads = keys.reshape(KEYS, HEAD_COUNT, HEAD_DIM).transpose(1, 0, 2)
    value_heads = values.reshape(KEYS, HEAD_COUNT, HEAD_DIM).transpose(1, 0, 2)

    def one_head(operands):
        query_part, key_part, value_part = operands
        scores = jnp.dot(query_part, key_part.T, preferred_element_type=jnp.float32)
        scores = jnp.where(valid, scores, floor_score)
        row_max = jnp.max(scores, axis=1, keepdims=True)
        terms = jnp.where(valid, jnp.exp(scores - row_max), 0.0)
        totals = jnp.sum(terms, axis=1, keepdims=True)
        summed = jnp.dot(terms.astype(jnp.bfloat16), value_part, preferred_element_type=jnp.float32)
        return (summed / totals).astype(jnp.bfloat16)

    attended = lax.map(one_head, (query_heads, key_heads, value_heads))
    attended = attended.transpose(1, 0, 2).reshape(ROWS, INNER)
    return jnp.dot(attended, out_weight, preferred_element_type=jnp.float32).astype(jnp.bfloat16)
```

```python
import functools

import jax
import jax.numpy as jnp
from jax import lax
from jax.experimental import pallas as pl
from jax.experimental.pallas import tpu as pltpu
from jax.sharding import PartitionSpec as P

HEAD_DIM = 64
PLEN = 256
BEAMS = 16
CHUNK = 256
CHUNK_HEADS = CHUNK // HEAD_DIM
LANES = 128
FLOOR = -1e30
MESH = pl.DeviceIdType.MESH
f32 = jnp.float32
bf16 = jnp.bfloat16


def diagonal(wide):
    head = lax.broadcasted_iota(jnp.int32, (BEAMS, CHUNK), 1) // HEAD_DIM
    result = wide[:BEAMS]
    for h in range(1, CHUNK_HEADS):
        result = jnp.where(head == h, wide[h * BEAMS:(h + 1) * BEAMS], result)
    return result


def kernel(n, nx, chunks, *refs):
    q_ref, k_ref, v_ref, w_ref, counts, slot_of, beam_request, out_ref = refs[:8]
    refs = refs[8:]

    def take():
        nonlocal refs
        mine, refs = refs[:chunks], refs[chunks:]
        return mine

    qall, kbuf, vbuf, wbuf, obuf, stats, dest, lbuf, rbuf = [take() for _ in range(9)]
    (pacc, s1, r1, s2, r2, load_sem, ag_send, ag_recv, st_send, st_recv,
     rs_send, rs_recv, x_send, x_recv) = refs

    rows = q_ref.shape[0]
    slots = k_ref.shape[0] // PLEN
    width = out_ref.shape[1]
    me = lax.axis_index("blk")
    hx = lax.axis_index("heads")
    sub = lax.axis_index("sub")
    at_left, at_right = me == 0, me == n - 1

    loads = {}
    for g in range(chunks):
        cols = pl.ds(g * CHUNK, CHUNK)
        for i, (src, dst) in enumerate(
            ((k_ref.at[:, cols], kbuf[g]), (v_ref.at[:, cols], vbuf[g]), (w_ref.at[cols, :], wbuf[g]))
        ):
            loads[g, i] = pltpu.make_async_copy(src, dst, load_sem.at[g, i])
    own_q = [
        pltpu.make_async_copy(
            q_ref.at[:, pl.ds(g * CHUNK, CHUNK)], qall[g].at[pl.ds(me * rows, rows), :], load_sem.at[g, 3]
        )
        for g in range(chunks)
    ]
    for g in range(chunks):
        own_q[g].start()
    for i in (0, 1):
        loads[0, i].start()

    barrier = pltpu.get_barrier_semaphore()
    for d in range(1, n):
        pl.semaphore_signal(barrier, inc=1, device_id={"blk": lax.rem(me + d, n)}, device_id_type=MESH)
    for d in range(1, nx):
        pl.semaphore_signal(barrier, inc=1, device_id={"heads": lax.rem(hx + d, nx)}, device_id_type=MESH)
    pl.semaphore_signal(barrier, inc=1, device_id={"sub": 1 - sub}, device_id_type=MESH)

    def ag_copy(g, origin, way, first=False):
        src = qall[g].at[pl.ds(origin * rows, rows), :]
        return pltpu.make_async_remote_copy(
            src_ref=src,
            dst_ref=qall[g].at[pl.ds(origin * rows, rows), :],
            send_sem=ag_send.at[g, origin, way],
            recv_sem=ag_recv.at[g, origin],
            device_id={"blk": me + 1 if way == 0 else me - 1},
            device_id_type=MESH,
        )

    pl.semaphore_wait(barrier, (n - 1) + (nx - 1) + 1)
    for g in range(chunks):
        own_q[g].wait()

        @pl.when(jnp.logical_not(at_right))
        def _():
            ag_copy(g, me, 0).start()

        @pl.when(jnp.logical_not(at_left))
        def _():
            ag_copy(g, me, 1).start()

    for g in range(chunks):
        for i in (0, 1):
            if g:
                loads[g, i].start()
    for g in range(chunks):
        loads[g, 2].start()

    def ag_service(g):
        for d in range(1, n):
            @pl.when(me - d >= 0)
            def _():
                ag_copy(g, me - d, 0).wait_recv()

                @pl.when(jnp.logical_not(at_right))
                def _():
                    ag_copy(g, me - d, 0).start()

            @pl.when(me + d < n)
            def _():
                ag_copy(g, me + d, 1).wait_recv()

                @pl.when(jnp.logical_not(at_left))
                def _():
                    ag_copy(g, me + d, 1).start()

    slot_col = lax.broadcasted_iota(jnp.int32, (n * slots, LANES), 0)
    passage_col = jnp.zeros((n * slots, LANES), jnp.int32)
    for p in range(n * slots):
        passage_col = jnp.where(slot_col == slot_of[p], p, passage_col)
    owner_col = jnp.zeros((n * slots, LANES), jnp.int32)
    end = jnp.int32(0)
    for r in range(counts.shape[0]):
        end = end + counts[r]
        owner_col = owner_col + jnp.where(passage_col >= end, 1, 0)
    beams_col = jnp.zeros((n * slots, LANES), jnp.int32)
    for i in range(beam_request.shape[0] // BEAMS):
        beams_col = jnp.where(owner_col == beam_request[i * BEAMS], i, beams_col)

    def slot_row(col, s):
        return jnp.sum(jnp.where(slot_col == me * slots + s, col, 0), axis=0, keepdims=True)

    owners = [slot_row(owner_col, s) for s in range(slots)]
    lane_row = lax.broadcasted_iota(jnp.int32, (1, slots * BEAMS), 1)
    target = jnp.zeros((1, slots * BEAMS), jnp.int32)
    for s in range(slots):
        target = jnp.where(lane_row // BEAMS == s, slot_row(beams_col, s) * BEAMS, target)
    target = target + lane_row % BEAMS
    scatter = jnp.where(
        lax.broadcasted_iota(jnp.int32, (n * rows, slots * BEAMS), 0) == target, 1.0, 0.0
    ).astype(bf16)

    block_mask = jnp.where(
        lax.broadcasted_iota(jnp.int32, (CHUNK_HEADS * BEAMS, CHUNK), 0) // BEAMS
        == lax.broadcasted_iota(jnp.int32, (CHUNK_HEADS * BEAMS, CHUNK), 1) // HEAD_DIM,
        1.0, 0.0,
    ).astype(bf16)
    stat_lane = lax.broadcasted_iota(jnp.int32, (CHUNK_HEADS * BEAMS, LANES), 1)

    def st_copy(g, origin, other):
        return pltpu.make_async_remote_copy(
            src_ref=stats[g].at[origin],
            dst_ref=stats[g].at[origin],
            send_sem=st_send.at[g, other],
            recv_sem=st_recv.at[g, origin],
            device_id={"blk": other},
            device_id_type=MESH,
        )

    def compute(g):
        loads[g, 0].wait()
        loads[g, 1].wait()
        picked = lax.dot_general(
            scatter, qall[g][...], (((0,), (0,)), ((), ())), preferred_element_type=f32
        ).astype(bf16)
        lse_all = jnp.zeros((CHUNK_HEADS * BEAMS, LANES), f32)
        for s in range(slots):
            q = jnp.concatenate([picked[s * BEAMS:(s + 1) * BEAMS]] * CHUNK_HEADS, axis=0) * block_mask
            keys = kbuf[g][pl.ds(s * PLEN, PLEN), :]
            scores = lax.dot_general(q, keys, (((1,), (1,)), ((), ())), preferred_element_type=f32)
            top = jnp.max(scores, axis=1, keepdims=True)
            terms = jnp.exp(scores - top)
            total = jnp.sum(terms, axis=1, keepdims=True)
            summed = jnp.dot(terms.astype(bf16), vbuf[g][pl.ds(s * PLEN, PLEN), :], preferred_element_type=f32)
            obuf[g][pl.ds(s * BEAMS, BEAMS), :] = diagonal(summed * (1.0 / total))
            lse_all = jnp.where(stat_lane == s, top + jnp.log(total), lse_all)
        turned = jnp.concatenate([lse_all] * (LANES // (CHUNK_HEADS * BEAMS)), axis=0).T
        stats[g][me] = turned[:slots]
        for d in range(1, n):
            st_copy(g, me, lax.rem(me + d, n)).start()

    def finish(g):
        for d in range(1, n):
            other = lax.rem(me + d, n)
            st_copy(g, other, other).wait_recv()
        every = stats[g][...].reshape(n * slots, LANES)
        own = stats[g][me]
        factors = []
        for s in range(slots):
            part = jnp.where(owner_col == owners[s], every, FLOOR)
            top = jnp.max(part, axis=0, keepdims=True)
            total = jnp.sum(jnp.exp(part - top), axis=0, keepdims=True)
            factors.append(jnp.exp(own[s:s + 1] - top) / total)
        factors.append(jnp.zeros((LANES - slots, LANES), f32))
        factors = jnp.concatenate(factors, axis=0).T
        scaled = []
        for s in range(slots):
            column = jnp.broadcast_to(factors[:CHUNK_HEADS * BEAMS, s:s + 1], (CHUNK_HEADS * BEAMS, CHUNK))
            scaled.append((obuf[g][pl.ds(s * BEAMS, BEAMS), :] * diagonal(column)).astype(bf16))
        scaled = jnp.concatenate(scaled, axis=0)
        moved = jnp.dot(scatter, scaled, preferred_element_type=f32)
        dest[g][...] = moved.astype(bf16).reshape(n, rows, CHUNK)

    def rs_copy(g, to, way):
        land = lbuf[g] if way == 0 else rbuf[g]
        return pltpu.make_async_remote_copy(
            src_ref=dest[g].at[to],
            dst_ref=land.at[to],
            send_sem=rs_send.at[g, to, way],
            recv_sem=rs_recv.at[g, to, way],
            device_id={"blk": me + 1 if way == 0 else me - 1},
            device_id_type=MESH,
        )

    def add_arrived(g, to, way):
        rs_copy(g, to, way).wait_recv()
        land = lbuf[g] if way == 0 else rbuf[g]
        dest[g][to] = (dest[g][to].astype(f32) + land[to].astype(f32)).astype(bf16)

    def rs_hop(g):
        for d in range(n - 1, 0, -1):
            @pl.when(me + d < n)
            def _():
                @pl.when(jnp.logical_not(at_left))
                def _():
                    add_arrived(g, me + d, 0)

                rs_copy(g, me + d, 0).start()

            @pl.when(me - d >= 0)
            def _():
                @pl.when(jnp.logical_not(at_right))
                def _():
                    add_arrived(g, me - d, 1)

                rs_copy(g, me - d, 1).start()

    def x_copy(stage, index, other):
        return pltpu.make_async_remote_copy(
            src_ref=(s1 if stage == 0 else s2).at[other],
            dst_ref=(r1 if stage == 0 else r2).at[index],
            send_sem=x_send.at[stage, other],
            recv_sem=x_recv.at[stage, index],
            device_id={"sub": 1 - sub} if stage == 0 else {"heads": other},
            device_id_type=MESH,
        )

    def project(g):
        @pl.when(jnp.logical_not(at_left))
        def _():
            add_arrived(g, me, 0)

        @pl.when(jnp.logical_not(at_right))
        def _():
            add_arrived(g, me, 1)

        loads[g, 2].wait()
        attended = dest[g][me]
        last = g == chunks - 1

        def column(h, sb):
            block = h * 2 + sb
            part = jnp.dot(
                attended, wbuf[g][:, pl.ds(pl.multiple_of(block * width, LANES), width)],
                preferred_element_type=f32,
            )
            if g:
                part = part + pacc[block]
            return part

        for d in list(range(1, nx)) + [0]:
            other = lax.rem(hx + d, nx)
            part = column(other, 1 - sub)
            if last:
                s1[other] = part.astype(bf16)
                x_copy(0, other, other).start()
            else:
                pacc[other * 2 + 1 - sub] = part
        for d in list(range(1, nx)) + [0]:
            other = lax.rem(hx + d, nx)
            pacc[other * 2 + sub] = column(other, sub)

    for step in range(chunks + 3):
        if step < chunks:
            ag_service(step)
            compute(step)
        if 0 <= step - 1 < chunks:
            finish(step - 1)
        if 0 <= step - 2 < chunks:
            rs_hop(step - 2)
        if 0 <= step - 3 < chunks:
            project(step - 3)

    for d in range(1, nx):
        other = lax.rem(hx + d, nx)
        x_copy(0, other, other).wait_recv()
        s2[other] = (pacc[other * 2 + sub] + r1[other].astype(f32)).astype(bf16)
        x_copy(1, hx, other).start()
    x_copy(0, hx, hx).wait_recv()
    result = pacc[hx * 2 + sub] + r1[hx].astype(f32)
    for d in range(1, nx):
        other = lax.rem(hx + d, nx)
        x_copy(1, other, other).wait_recv()
        result = result + r2[other].astype(f32)
    out_ref[...] = result.astype(bf16)

    for g in range(chunks):
        for o in range(n):
            @pl.when(jnp.logical_and(o <= me, jnp.logical_not(at_right)))
            def _():
                ag_copy(g, o, 0).wait_send()

            @pl.when(jnp.logical_and(o >= me, jnp.logical_not(at_left)))
            def _():
                ag_copy(g, o, 1).wait_send()

            @pl.when(me < o)
            def _():
                rs_copy(g, o, 0).wait_send()

            @pl.when(me > o)
            def _():
                rs_copy(g, o, 1).wait_send()

        for d in range(1, n):
            st_copy(g, me, lax.rem(me + d, n)).wait_send()
    for h in range(nx):
        x_copy(0, h, h).wait_send()
    for d in range(1, nx):
        x_copy(1, hx, lax.rem(hx + d, nx)).wait_send()


def body(n, nx, queries, keys, values, out_weight, counts, slot_of, beam_request):
    rows, features = queries.shape
    chunks = features // CHUNK
    slots = keys.shape[0] // PLEN
    columns = out_weight.shape[1]
    width = columns // (nx * 2)
    dma = pltpu.SemaphoreType.DMA

    def per_chunk(shape, dtype):
        return [pltpu.VMEM(shape, dtype) for _ in range(chunks)]

    smem = pl.BlockSpec(memory_space=pltpu.SMEM)
    hbm = pl.BlockSpec(memory_space=pl.ANY)
    return pl.pallas_call(
        functools.partial(kernel, n, nx, chunks),
        out_shape=jax.ShapeDtypeStruct((rows, width), bf16),
        in_specs=[hbm] * 4 + [smem] * 3,
        out_specs=pl.BlockSpec(memory_space=pltpu.VMEM),
        scratch_shapes=(
            per_chunk((n * rows, CHUNK), bf16)
            + per_chunk((keys.shape[0], CHUNK), bf16)
            + per_chunk((keys.shape[0], CHUNK), bf16)
            + per_chunk((CHUNK, columns), bf16)
            + per_chunk((slots * BEAMS, CHUNK), f32)
            + per_chunk((n, slots, LANES), f32)
            + per_chunk((n, rows, CHUNK), bf16)
            + per_chunk((n, rows, CHUNK), bf16)
            + per_chunk((n, rows, CHUNK), bf16)
            + [
                pltpu.VMEM((nx * 2, rows, width), f32),
                pltpu.VMEM((nx, rows, width), bf16),
                pltpu.VMEM((nx, rows, width), bf16),
                pltpu.VMEM((nx, rows, width), bf16),
                pltpu.VMEM((nx, rows, width), bf16),
                dma((chunks, 4)),
                dma((chunks, n, 2)),
                dma((chunks, n)),
                dma((chunks, n)),
                dma((chunks, n)),
                dma((chunks, n, 2)),
                dma((chunks, n, 2)),
                dma((2, nx)),
                dma((2, nx)),
            ]
        ),
        compiler_params=pltpu.CompilerParams(
            collective_id=0, has_side_effects=True, vmem_limit_bytes=48 * 1024 * 1024
        ),
    )(queries, keys, values, out_weight, counts, slot_of, beam_request)


def solution(mesh):
    return jax.shard_map(
        functools.partial(body, mesh.shape["blk"], mesh.shape["heads"]),
        mesh=mesh,
        in_specs=(
            P(("groups", "blk"), ("heads", "sub")),
            P(("groups", "blk"), ("heads", "sub")),
            P(("groups", "blk"), ("heads", "sub")),
            P(("heads", "sub"), None),
            P("groups"),
            P("groups"),
            P("groups"),
        ),
        out_specs=P(("groups", "blk"), ("heads", "sub")),
        check_vma=False,
    )
```

```python
import functools

import jax
import jax.numpy as jnp
from jax import lax
from jax.experimental import pallas as pl
from jax.experimental.pallas import tpu as pltpu
from jax.sharding import PartitionSpec as P

HEAD_DIM = 64
PLEN = 256
BEAMS = 16
CHUNK = 256
CHUNK_HEADS = CHUNK // HEAD_DIM
LANES = 128
FLOOR = -1e30
MESH = pl.DeviceIdType.MESH
f32 = jnp.float32
bf16 = jnp.bfloat16


def diagonal(wide):
    head = lax.broadcasted_iota(jnp.int32, (BEAMS, CHUNK), 1) // HEAD_DIM
    result = wide[:BEAMS]
    for h in range(1, CHUNK_HEADS):
        result = jnp.where(head == h, wide[h * BEAMS:(h + 1) * BEAMS], result)
    return result


def kernel(n, nx, chunks, *refs):
    q_ref, k_ref, v_ref, w_ref, counts, slot_of, beam_request, out_ref = refs[:8]
    refs = refs[8:]

    def take():
        nonlocal refs
        mine, refs = refs[:chunks], refs[chunks:]
        return mine

    qall, kbuf, vbuf, wbuf, obuf, stats, dest, land = [take() for _ in range(8)]
    (pacc, s1, r1, s2, r2, load_sem, ag_send, ag_recv, st_send, st_recv,
     rs_send, rs_recv, x_send, x_recv) = refs

    rows = q_ref.shape[0]
    slots = k_ref.shape[0] // PLEN
    width = out_ref.shape[1]
    me = lax.axis_index("blk")
    hx = lax.axis_index("heads")
    sub = lax.axis_index("sub")

    loads = {}
    for g in range(chunks):
        cols = pl.ds(g * CHUNK, CHUNK)
        for i, (src, dst) in enumerate(
            ((k_ref.at[:, cols], kbuf[g]), (v_ref.at[:, cols], vbuf[g]), (w_ref.at[cols, :], wbuf[g]))
        ):
            loads[g, i] = pltpu.make_async_copy(src, dst, load_sem.at[g, i])
    own_q = [
        pltpu.make_async_copy(
            q_ref.at[:, pl.ds(g * CHUNK, CHUNK)], qall[g].at[pl.ds(me * rows, rows), :], load_sem.at[g, 3]
        )
        for g in range(chunks)
    ]
    for g in range(chunks):
        own_q[g].start()
    for i in (0, 1):
        loads[0, i].start()

    barrier = pltpu.get_barrier_semaphore()
    for d in range(1, n):
        pl.semaphore_signal(barrier, inc=1, device_id={"blk": lax.rem(me + d, n)}, device_id_type=MESH)
    for d in range(1, nx):
        pl.semaphore_signal(barrier, inc=1, device_id={"heads": lax.rem(hx + d, nx)}, device_id_type=MESH)
    pl.semaphore_signal(barrier, inc=1, device_id={"sub": 1 - sub}, device_id_type=MESH)

    def ag_copy(g, origin, to):
        rows_there = pl.ds(origin * rows, rows)
        return pltpu.make_async_remote_copy(
            src_ref=qall[g].at[rows_there, :],
            dst_ref=qall[g].at[rows_there, :],
            send_sem=ag_send.at[g, to],
            recv_sem=ag_recv.at[g, origin],
            device_id={"blk": to},
            device_id_type=MESH,
        )

    pl.semaphore_wait(barrier, (n - 1) + (nx - 1) + 1)
    for g in range(chunks):
        own_q[g].wait()

        for d in range(1, n):
            ag_copy(g, me, lax.rem(me + d, n)).start()

    for g in range(chunks):
        for i in (0, 1):
            if g:
                loads[g, i].start()
    for g in range(chunks):
        loads[g, 2].start()

    def ag_service(g):
        for d in range(1, n):
            other = lax.rem(me + d, n)
            ag_copy(g, other, other).wait_recv()

    slot_col = lax.broadcasted_iota(jnp.int32, (n * slots, LANES), 0)
    passage_col = jnp.zeros((n * slots, LANES), jnp.int32)
    for p in range(n * slots):
        passage_col = jnp.where(slot_col == slot_of[p], p, passage_col)
    owner_col = jnp.zeros((n * slots, LANES), jnp.int32)
    end = jnp.int32(0)
    for r in range(counts.shape[0]):
        end = end + counts[r]
        owner_col = owner_col + jnp.where(passage_col >= end, 1, 0)
    beams_col = jnp.zeros((n * slots, LANES), jnp.int32)
    for i in range(beam_request.shape[0] // BEAMS):
        beams_col = jnp.where(owner_col == beam_request[i * BEAMS], i, beams_col)

    def slot_row(col, s):
        return jnp.sum(jnp.where(slot_col == me * slots + s, col, 0), axis=0, keepdims=True)

    owners = [slot_row(owner_col, s) for s in range(slots)]
    lane_row = lax.broadcasted_iota(jnp.int32, (1, slots * BEAMS), 1)
    target = jnp.zeros((1, slots * BEAMS), jnp.int32)
    for s in range(slots):
        target = jnp.where(lane_row // BEAMS == s, slot_row(beams_col, s) * BEAMS, target)
    target = target + lane_row % BEAMS
    scatter = jnp.where(
        lax.broadcasted_iota(jnp.int32, (n * rows, slots * BEAMS), 0) == target, 1.0, 0.0
    ).astype(bf16)

    block_mask = jnp.where(
        lax.broadcasted_iota(jnp.int32, (CHUNK_HEADS * BEAMS, CHUNK), 0) // BEAMS
        == lax.broadcasted_iota(jnp.int32, (CHUNK_HEADS * BEAMS, CHUNK), 1) // HEAD_DIM,
        1.0, 0.0,
    ).astype(bf16)
    stat_lane = lax.broadcasted_iota(jnp.int32, (CHUNK_HEADS * BEAMS, LANES), 1)

    def st_copy(g, origin, other):
        return pltpu.make_async_remote_copy(
            src_ref=stats[g].at[origin],
            dst_ref=stats[g].at[origin],
            send_sem=st_send.at[g, other],
            recv_sem=st_recv.at[g, origin],
            device_id={"blk": other},
            device_id_type=MESH,
        )

    def compute(g):
        loads[g, 0].wait()
        loads[g, 1].wait()
        picked = lax.dot_general(
            scatter, qall[g][...], (((0,), (0,)), ((), ())), preferred_element_type=f32
        ).astype(bf16)
        lse_all = jnp.zeros((CHUNK_HEADS * BEAMS, LANES), f32)
        for s in range(slots):
            q = jnp.concatenate([picked[s * BEAMS:(s + 1) * BEAMS]] * CHUNK_HEADS, axis=0) * block_mask
            keys = kbuf[g][pl.ds(s * PLEN, PLEN), :]
            scores = lax.dot_general(q, keys, (((1,), (1,)), ((), ())), preferred_element_type=f32)
            top = jnp.max(scores, axis=1, keepdims=True)
            terms = jnp.exp(scores - top)
            total = jnp.sum(terms, axis=1, keepdims=True)
            summed = jnp.dot(terms.astype(bf16), vbuf[g][pl.ds(s * PLEN, PLEN), :], preferred_element_type=f32)
            obuf[g][pl.ds(s * BEAMS, BEAMS), :] = diagonal(summed * (1.0 / total))
            lse_all = jnp.where(stat_lane == s, top + jnp.log(total), lse_all)
        turned = jnp.concatenate([lse_all] * (LANES // (CHUNK_HEADS * BEAMS)), axis=0).T
        stats[g][me] = turned[:slots]
        for d in range(1, n):
            st_copy(g, me, lax.rem(me + d, n)).start()

    def finish(g):
        for d in range(1, n):
            other = lax.rem(me + d, n)
            st_copy(g, other, other).wait_recv()
        every = stats[g][...].reshape(n * slots, LANES)
        own = stats[g][me]
        factors = []
        for s in range(slots):
            part = jnp.where(owner_col == owners[s], every, FLOOR)
            top = jnp.max(part, axis=0, keepdims=True)
            total = jnp.sum(jnp.exp(part - top), axis=0, keepdims=True)
            factors.append(jnp.exp(own[s:s + 1] - top) / total)
        factors.append(jnp.zeros((LANES - slots, LANES), f32))
        factors = jnp.concatenate(factors, axis=0).T
        scaled = []
        for s in range(slots):
            column = jnp.broadcast_to(factors[:CHUNK_HEADS * BEAMS, s:s + 1], (CHUNK_HEADS * BEAMS, CHUNK))
            scaled.append((obuf[g][pl.ds(s * BEAMS, BEAMS), :] * diagonal(column)).astype(bf16))
        scaled = jnp.concatenate(scaled, axis=0)
        moved = jnp.dot(scatter, scaled, preferred_element_type=f32)
        dest[g][...] = moved.astype(bf16).reshape(n, rows, CHUNK)

    def rs_copy(g, index, other):
        return pltpu.make_async_remote_copy(
            src_ref=dest[g].at[other],
            dst_ref=land[g].at[index],
            send_sem=rs_send.at[g, other],
            recv_sem=rs_recv.at[g, index],
            device_id={"blk": other},
            device_id_type=MESH,
        )

    def rs_start(g):
        for d in range(1, n):
            rs_copy(g, me, lax.rem(me + d, n)).start()

    def x_copy(stage, index, other):
        return pltpu.make_async_remote_copy(
            src_ref=(s1 if stage == 0 else s2).at[other],
            dst_ref=(r1 if stage == 0 else r2).at[index],
            send_sem=x_send.at[stage, other],
            recv_sem=x_recv.at[stage, index],
            device_id={"sub": 1 - sub} if stage == 0 else {"heads": other},
            device_id_type=MESH,
        )

    def project(g):
        attended = dest[g][me].astype(f32)
        for d in range(1, n):
            other = lax.rem(me + d, n)
            rs_copy(g, other, other).wait_recv()
            attended = attended + land[g][other].astype(f32)
        attended = attended.astype(bf16)
        loads[g, 2].wait()
        last = g == chunks - 1

        def column(h, sb):
            block = h * 2 + sb
            part = jnp.dot(
                attended, wbuf[g][:, pl.ds(pl.multiple_of(block * width, LANES), width)],
                preferred_element_type=f32,
            )
            if g:
                part = part + pacc[block]
            return part

        for d in list(range(1, nx)) + [0]:
            other = lax.rem(hx + d, nx)
            part = column(other, 1 - sub)
            if last:
                s1[other] = part.astype(bf16)
                x_copy(0, other, other).start()
            else:
                pacc[other * 2 + 1 - sub] = part
        for d in list(range(1, nx)) + [0]:
            other = lax.rem(hx + d, nx)
            pacc[other * 2 + sub] = column(other, sub)

    for step in range(chunks + 3):
        if step < chunks:
            ag_service(step)
            compute(step)
        if 0 <= step - 1 < chunks:
            finish(step - 1)
            rs_start(step - 1)
        if 0 <= step - 3 < chunks:
            project(step - 3)

    for d in range(1, nx):
        other = lax.rem(hx + d, nx)
        x_copy(0, other, other).wait_recv()
        s2[other] = (pacc[other * 2 + sub] + r1[other].astype(f32)).astype(bf16)
        x_copy(1, hx, other).start()
    x_copy(0, hx, hx).wait_recv()
    result = pacc[hx * 2 + sub] + r1[hx].astype(f32)
    for d in range(1, nx):
        other = lax.rem(hx + d, nx)
        x_copy(1, other, other).wait_recv()
        result = result + r2[other].astype(f32)
    out_ref[...] = result.astype(bf16)

    for g in range(chunks):
        for d in range(1, n):
            other = lax.rem(me + d, n)
            ag_copy(g, me, other).wait_send()
            st_copy(g, me, other).wait_send()
            rs_copy(g, me, other).wait_send()
    for h in range(nx):
        x_copy(0, h, h).wait_send()
    for d in range(1, nx):
        x_copy(1, hx, lax.rem(hx + d, nx)).wait_send()


def body(n, nx, queries, keys, values, out_weight, counts, slot_of, beam_request):
    rows, features = queries.shape
    chunks = features // CHUNK
    slots = keys.shape[0] // PLEN
    columns = out_weight.shape[1]
    width = columns // (nx * 2)
    dma = pltpu.SemaphoreType.DMA

    def per_chunk(shape, dtype):
        return [pltpu.VMEM(shape, dtype) for _ in range(chunks)]

    smem = pl.BlockSpec(memory_space=pltpu.SMEM)
    hbm = pl.BlockSpec(memory_space=pl.ANY)
    return pl.pallas_call(
        functools.partial(kernel, n, nx, chunks),
        out_shape=jax.ShapeDtypeStruct((rows, width), bf16),
        in_specs=[hbm] * 4 + [smem] * 3,
        out_specs=pl.BlockSpec(memory_space=pltpu.VMEM),
        scratch_shapes=(
            per_chunk((n * rows, CHUNK), bf16)
            + per_chunk((keys.shape[0], CHUNK), bf16)
            + per_chunk((keys.shape[0], CHUNK), bf16)
            + per_chunk((CHUNK, columns), bf16)
            + per_chunk((slots * BEAMS, CHUNK), f32)
            + per_chunk((n, slots, LANES), f32)
            + per_chunk((n, rows, CHUNK), bf16)
            + per_chunk((n, rows, CHUNK), bf16)
            + [
                pltpu.VMEM((nx * 2, rows, width), f32),
                pltpu.VMEM((nx, rows, width), bf16),
                pltpu.VMEM((nx, rows, width), bf16),
                pltpu.VMEM((nx, rows, width), bf16),
                pltpu.VMEM((nx, rows, width), bf16),
                dma((chunks, 4)),
                dma((chunks, n)),
                dma((chunks, n)),
                dma((chunks, n)),
                dma((chunks, n)),
                dma((chunks, n)),
                dma((chunks, n)),
                dma((2, nx)),
                dma((2, nx)),
            ]
        ),
        compiler_params=pltpu.CompilerParams(
            collective_id=0, has_side_effects=True, vmem_limit_bytes=60 * 1024 * 1024
        ),
    )(queries, keys, values, out_weight, counts, slot_of, beam_request)


def solution(mesh):
    return jax.shard_map(
        functools.partial(body, mesh.shape["blk"], mesh.shape["heads"]),
        mesh=mesh,
        in_specs=(
            P(("groups", "blk"), ("heads", "sub")),
            P(("groups", "blk"), ("heads", "sub")),
            P(("groups", "blk"), ("heads", "sub")),
            P(("heads", "sub"), None),
            P("groups"),
            P("groups"),
            P("groups"),
        ),
        out_specs=P(("groups", "blk"), ("heads", "sub")),
        check_vma=False,
    )
```

```python
import functools

import jax
import jax.numpy as jnp
from jax import lax
from jax.experimental import pallas as pl
from jax.experimental.pallas import tpu as pltpu
from jax.sharding import PartitionSpec as P

HEAD_DIM = 64
PLEN = 256
BEAMS = 16
CHUNK = 256
CHUNK_HEADS = CHUNK // HEAD_DIM
LANES = 128
FLOOR = -1e30
MESH = pl.DeviceIdType.MESH
f32 = jnp.float32
bf16 = jnp.bfloat16


def diagonal(wide):
    head = lax.broadcasted_iota(jnp.int32, (BEAMS, CHUNK), 1) // HEAD_DIM
    result = wide[:BEAMS]
    for h in range(1, CHUNK_HEADS):
        result = jnp.where(head == h, wide[h * BEAMS:(h + 1) * BEAMS], result)
    return result


def kernel(n, nx, chunks, *refs):
    q_ref, k_ref, v_ref, w_ref, counts, slot_of, beam_request, out_ref = refs[:8]
    refs = refs[8:]

    def take():
        nonlocal refs
        mine, refs = refs[:chunks], refs[chunks:]
        return mine

    qall, kbuf, vbuf, wbuf, obuf, stats, dest, land = [take() for _ in range(8)]
    (pacc, s1, r1, s2, r2, load_sem, ag_send, ag_recv, st_send, st_recv,
     rs_send, rs_recv, x_send, x_recv) = refs

    rows = q_ref.shape[0]
    slots = k_ref.shape[0] // PLEN
    width = out_ref.shape[1]
    me = lax.axis_index("blk")
    hx = lax.axis_index("heads")
    sub = lax.axis_index("sub")

    loads = {}
    for g in range(chunks):
        cols = pl.ds(g * CHUNK, CHUNK)
        for i, (src, dst) in enumerate(
            ((k_ref.at[:, cols], kbuf[g]), (v_ref.at[:, cols], vbuf[g]), (w_ref.at[cols, :], wbuf[g]))
        ):
            loads[g, i] = pltpu.make_async_copy(src, dst, load_sem.at[g, i])
    own_q = [
        pltpu.make_async_copy(
            q_ref.at[:, pl.ds(g * CHUNK, CHUNK)], qall[g].at[pl.ds(me * rows, rows), :], load_sem.at[g, 3]
        )
        for g in range(chunks)
    ]
    for g in range(chunks):
        own_q[g].start()
    for i in (0, 1):
        loads[0, i].start()

    barrier = pltpu.get_barrier_semaphore()
    for d in range(1, n):
        pl.semaphore_signal(barrier, inc=1, device_id={"blk": lax.rem(me + d, n)}, device_id_type=MESH)
    for d in range(1, nx):
        pl.semaphore_signal(barrier, inc=1, device_id={"heads": lax.rem(hx + d, nx)}, device_id_type=MESH)
    pl.semaphore_signal(barrier, inc=1, device_id={"sub": 1 - sub}, device_id_type=MESH)

    def ag_copy(g, origin, to):
        rows_there = pl.ds(origin * rows, rows)
        return pltpu.make_async_remote_copy(
            src_ref=qall[g].at[rows_there, :],
            dst_ref=qall[g].at[rows_there, :],
            send_sem=ag_send.at[g, to],
            recv_sem=ag_recv.at[g, origin],
            device_id={"blk": to},
            device_id_type=MESH,
        )

    pl.semaphore_wait(barrier, (n - 1) + (nx - 1) + 1)
    for g in range(chunks):
        own_q[g].wait()

        for d in range(1, n):
            ag_copy(g, me, lax.rem(me + d, n)).start()

    for g in range(chunks):
        for i in (0, 1):
            if g:
                loads[g, i].start()
    for g in range(chunks):
        loads[g, 2].start()

    def ag_service(g):
        for d in range(1, n):
            other = lax.rem(me + d, n)
            ag_copy(g, other, other).wait_recv()

    slot_col = lax.broadcasted_iota(jnp.int32, (n * slots, LANES), 0)
    passage_col = jnp.zeros((n * slots, LANES), jnp.int32)
    for p in range(n * slots):
        passage_col = jnp.where(slot_col == slot_of[p], p, passage_col)
    owner_col = jnp.zeros((n * slots, LANES), jnp.int32)
    end = jnp.int32(0)
    for r in range(counts.shape[0]):
        end = end + counts[r]
        owner_col = owner_col + jnp.where(passage_col >= end, 1, 0)
    beams_col = jnp.zeros((n * slots, LANES), jnp.int32)
    for i in range(beam_request.shape[0] // BEAMS):
        beams_col = jnp.where(owner_col == beam_request[i * BEAMS], i, beams_col)

    def slot_row(col, s):
        return jnp.sum(jnp.where(slot_col == me * slots + s, col, 0), axis=0, keepdims=True)

    owners = [slot_row(owner_col, s) for s in range(slots)]
    lane_row = lax.broadcasted_iota(jnp.int32, (1, slots * BEAMS), 1)
    target = jnp.zeros((1, slots * BEAMS), jnp.int32)
    for s in range(slots):
        target = jnp.where(lane_row // BEAMS == s, slot_row(beams_col, s) * BEAMS, target)
    target = target + lane_row % BEAMS
    scatter = jnp.where(
        lax.broadcasted_iota(jnp.int32, (n * rows, slots * BEAMS), 0) == target, 1.0, 0.0
    ).astype(bf16)

    block_mask = jnp.where(
        lax.broadcasted_iota(jnp.int32, (CHUNK_HEADS * BEAMS, CHUNK), 0) // BEAMS
        == lax.broadcasted_iota(jnp.int32, (CHUNK_HEADS * BEAMS, CHUNK), 1) // HEAD_DIM,
        1.0, 0.0,
    ).astype(bf16)
    stat_lane = lax.broadcasted_iota(jnp.int32, (CHUNK_HEADS * BEAMS, LANES), 1)

    def st_copy(g, origin, other):
        return pltpu.make_async_remote_copy(
            src_ref=stats[g].at[origin],
            dst_ref=stats[g].at[origin],
            send_sem=st_send.at[g, other],
            recv_sem=st_recv.at[g, origin],
            device_id={"blk": other},
            device_id_type=MESH,
        )

    def compute(g):
        loads[g, 0].wait()
        loads[g, 1].wait()
        picked = lax.dot_general(
            scatter, qall[g][...], (((0,), (0,)), ((), ())), preferred_element_type=f32
        ).astype(bf16)
        lse_all = jnp.zeros((CHUNK_HEADS * BEAMS, LANES), f32)
        for s in range(slots):
            q = jnp.concatenate([picked[s * BEAMS:(s + 1) * BEAMS]] * CHUNK_HEADS, axis=0) * block_mask
            keys = kbuf[g][pl.ds(s * PLEN, PLEN), :]
            scores = lax.dot_general(q, keys, (((1,), (1,)), ((), ())), preferred_element_type=f32)
            top = jnp.max(scores, axis=1, keepdims=True)
            terms = jnp.exp(scores - top)
            total = jnp.sum(terms, axis=1, keepdims=True)
            summed = jnp.dot(terms.astype(bf16), vbuf[g][pl.ds(s * PLEN, PLEN), :], preferred_element_type=f32)
            obuf[g][pl.ds(s * BEAMS, BEAMS), :] = diagonal(summed * (1.0 / total))
            lse_all = jnp.where(stat_lane == s, top + jnp.log(total), lse_all)
        turned = jnp.concatenate([lse_all] * (LANES // (CHUNK_HEADS * BEAMS)), axis=0).T
        stats[g][me] = turned[:slots]
        for d in range(1, n):
            st_copy(g, me, lax.rem(me + d, n)).start()

    def finish(g):
        for d in range(1, n):
            other = lax.rem(me + d, n)
            st_copy(g, other, other).wait_recv()
        every = stats[g][...].reshape(n * slots, LANES)
        own = stats[g][me]
        factors = []
        for s in range(slots):
            part = jnp.where(owner_col == owners[s], every, FLOOR)
            top = jnp.max(part, axis=0, keepdims=True)
            total = jnp.sum(jnp.exp(part - top), axis=0, keepdims=True)
            factors.append(jnp.exp(own[s:s + 1] - top) / total)
        factors.append(jnp.zeros((LANES - slots, LANES), f32))
        factors = jnp.concatenate(factors, axis=0).T
        scaled = []
        for s in range(slots):
            column = jnp.broadcast_to(factors[:CHUNK_HEADS * BEAMS, s:s + 1], (CHUNK_HEADS * BEAMS, CHUNK))
            scaled.append((obuf[g][pl.ds(s * BEAMS, BEAMS), :] * diagonal(column)).astype(bf16))
        scaled = jnp.concatenate(scaled, axis=0)
        moved = jnp.dot(scatter, scaled, preferred_element_type=f32)
        dest[g][...] = moved.astype(bf16).reshape(n, rows, CHUNK)

    def rs_copy(g, index, other):
        return pltpu.make_async_remote_copy(
            src_ref=dest[g].at[other],
            dst_ref=land[g].at[index],
            send_sem=rs_send.at[g, other],
            recv_sem=rs_recv.at[g, index],
            device_id={"blk": other},
            device_id_type=MESH,
        )

    def rs_start(g):
        for d in range(1, n):
            rs_copy(g, me, lax.rem(me + d, n)).start()

    def x_copy(stage, index, other):
        return pltpu.make_async_remote_copy(
            src_ref=(s1 if stage == 0 else s2).at[other],
            dst_ref=(r1 if stage == 0 else r2).at[index],
            send_sem=x_send.at[stage, other],
            recv_sem=x_recv.at[stage, index],
            device_id={"sub": 1 - sub} if stage == 0 else {"heads": other},
            device_id_type=MESH,
        )

    def project(g):
        attended = dest[g][me].astype(f32)
        for d in range(1, n):
            other = lax.rem(me + d, n)
            rs_copy(g, other, other).wait_recv()
            attended = attended + land[g][other].astype(f32)
        attended = attended.astype(bf16)
        loads[g, 2].wait()
        last = g == chunks - 1

        def column(h, sb):
            block = h * 2 + sb
            part = jnp.dot(
                attended, wbuf[g][:, pl.ds(pl.multiple_of(block * width, LANES), width)],
                preferred_element_type=f32,
            )
            if g:
                part = part + pacc[block]
            return part

        for d in list(range(1, nx)) + [0]:
            other = lax.rem(hx + d, nx)
            part = column(other, 1 - sub)
            if last:
                s1[other] = part.astype(bf16)
                x_copy(0, other, other).start()
            else:
                pacc[other * 2 + 1 - sub] = part
        for d in list(range(1, nx)) + [0]:
            other = lax.rem(hx + d, nx)
            pacc[other * 2 + sub] = column(other, sub)

    for step in range(chunks + 4):
        if step < chunks:
            ag_service(step)
            compute(step)
        if 0 <= step - 1 < chunks:
            finish(step - 1)
            rs_start(step - 1)
        if 0 <= step - 4 < chunks:
            project(step - 4)

    for d in range(1, nx):
        other = lax.rem(hx + d, nx)
        x_copy(0, other, other).wait_recv()
        s2[other] = (pacc[other * 2 + sub] + r1[other].astype(f32)).astype(bf16)
        x_copy(1, hx, other).start()
    x_copy(0, hx, hx).wait_recv()
    result = pacc[hx * 2 + sub] + r1[hx].astype(f32)
    for d in range(1, nx):
        other = lax.rem(hx + d, nx)
        x_copy(1, other, other).wait_recv()
        result = result + r2[other].astype(f32)
    out_ref[...] = result.astype(bf16)

    for g in range(chunks):
        for d in range(1, n):
            other = lax.rem(me + d, n)
            ag_copy(g, me, other).wait_send()
            st_copy(g, me, other).wait_send()
            rs_copy(g, me, other).wait_send()
    for h in range(nx):
        x_copy(0, h, h).wait_send()
    for d in range(1, nx):
        x_copy(1, hx, lax.rem(hx + d, nx)).wait_send()


def body(n, nx, queries, keys, values, out_weight, counts, slot_of, beam_request):
    rows, features = queries.shape
    chunks = features // CHUNK
    slots = keys.shape[0] // PLEN
    columns = out_weight.shape[1]
    width = columns // (nx * 2)
    dma = pltpu.SemaphoreType.DMA

    def per_chunk(shape, dtype):
        return [pltpu.VMEM(shape, dtype) for _ in range(chunks)]

    smem = pl.BlockSpec(memory_space=pltpu.SMEM)
    hbm = pl.BlockSpec(memory_space=pl.ANY)
    return pl.pallas_call(
        functools.partial(kernel, n, nx, chunks),
        out_shape=jax.ShapeDtypeStruct((rows, width), bf16),
        in_specs=[hbm] * 4 + [smem] * 3,
        out_specs=pl.BlockSpec(memory_space=pltpu.VMEM),
        scratch_shapes=(
            per_chunk((n * rows, CHUNK), bf16)
            + per_chunk((keys.shape[0], CHUNK), bf16)
            + per_chunk((keys.shape[0], CHUNK), bf16)
            + per_chunk((CHUNK, columns), bf16)
            + per_chunk((slots * BEAMS, CHUNK), f32)
            + per_chunk((n, slots, LANES), f32)
            + per_chunk((n, rows, CHUNK), bf16)
            + per_chunk((n, rows, CHUNK), bf16)
            + [
                pltpu.VMEM((nx * 2, rows, width), f32),
                pltpu.VMEM((nx, rows, width), bf16),
                pltpu.VMEM((nx, rows, width), bf16),
                pltpu.VMEM((nx, rows, width), bf16),
                pltpu.VMEM((nx, rows, width), bf16),
                dma((chunks, 4)),
                dma((chunks, n)),
                dma((chunks, n)),
                dma((chunks, n)),
                dma((chunks, n)),
                dma((chunks, n)),
                dma((chunks, n)),
                dma((2, nx)),
                dma((2, nx)),
            ]
        ),
        compiler_params=pltpu.CompilerParams(
            collective_id=0, has_side_effects=True, vmem_limit_bytes=60 * 1024 * 1024
        ),
    )(queries, keys, values, out_weight, counts, slot_of, beam_request)


def solution(mesh):
    return jax.shard_map(
        functools.partial(body, mesh.shape["blk"], mesh.shape["heads"]),
        mesh=mesh,
        in_specs=(
            P(("groups", "blk"), ("heads", "sub")),
            P(("groups", "blk"), ("heads", "sub")),
            P(("groups", "blk"), ("heads", "sub")),
            P(("heads", "sub"), None),
            P("groups"),
            P("groups"),
            P("groups"),
        ),
        out_specs=P(("groups", "blk"), ("heads", "sub")),
        check_vma=False,
    )
```
